32 devices in a mesh: row: 4 (over y, x), col: 8 (over z, core).
Axes of the slice: x: 2, y: 2, z: 4, core: 2. Of those that a mesh axis runs over, the one named last changes fastest.
Arguments:
- factors: bfloat16 [10240, 3, 2048], P(('row', 'col')), may hold values from -0.59765625 to 0.59765625
- occ_energy: float32 [300], replicated, may hold values from -3 to -0.5
- vir_energy: float32 [2048], replicated, may hold values from 0.3 to 4
- slab_orbitals: int32 [3], replicated, may hold values from 0 to 299
- pair_list: int32 [16, 2], replicated, may hold values from 0 to 2
- pair_state: int32 [16], replicated, may hold values from 0 to 3
- state_shift: float32 [4], replicated, may hold values from 0.1 to 1
Outputs:
- amplitudes: float32 [16, 2048, 2048], P(None, 'row', 'col')
The draws below stay inside these ranges and needn't reach their ends.
All inputs are finite; a program needn't handle non-finite values.
Results may differ from the reference program's by a relative error of at most 0.0003.
Values may be sent and summed in bfloat16 or wider, within the bound.
A program may use at most 192 MiB of HBM per device.

```python
import math
import jax
import jax.numpy as jnp
from jax import lax

NAUX = 10240
NV = 2048
NCORE = 300
NOCC = 3
NPAIR = 16
NSTATE = 4


def place_ends(entries, key, low, top_value):
    index_at = [jax.random.randint(jax.random.fold_in(key, axis), (), 0, length) for axis, length in enumerate(entries.shape)]
    main_axis = entries.shape.index(max(entries.shape))
    beside = index_at[:main_axis] + [(index_at[main_axis] + 1) % entries.shape[main_axis]] + index_at[main_axis + 1:]
    return entries.at[tuple(index_at)].set(low).at[tuple(beside)].set(top_value)


def block_levels(key, shape, split, smallest, top_value):
    def one(axis_at, shards_of):
        heights = jax.random.uniform(jax.random.fold_in(jax.random.fold_in(key, 6), axis_at), (shards_of,), jnp.float32, smallest / len(split), top_value / len(split))
        return jnp.repeat(jnp.exp(heights), shape[axis_at] // shards_of).reshape((-1,) + (1,) * (len(shape) - axis_at - 1))

    loudness = one(*split[0])
    for cut in split[1:]:
        loudness = loudness * one(*cut)
    return loudness


def normal_values(rng, dims, width, reach, pieces=(), dtype=jnp.bfloat16):
    loudness = block_levels(rng, dims, pieces, -0.22, 0.18) if pieces else 1.0
    drawn = jax.random.normal(rng, dims, jnp.float32) * width * loudness
    return jnp.minimum(jnp.maximum(drawn, -reach), reach).astype(dtype)


def setup_inputs(seed: int = 0) -> dict:
    splits = jax.random.split(jax.random.key(seed), 8)
    return {
        "factors": normal_values(splits[0], (NAUX, NOCC, NV), 0.1, 0.59765625, ((0, 32),)),
        "occ_energy": jnp.clip(jax.random.uniform(splits[1], (NCORE,), jnp.float32, -3.0, -0.5), -3.0, -0.5),
        "vir_energy": jnp.clip(jax.random.uniform(splits[2], (NV,), jnp.float32, 0.3, 4.0), 0.3, 4.0),
        "slab_orbitals": jax.random.randint(splits[3], (NOCC,), 0, NCORE).astype(jnp.int32),
        "pair_list": place_ends(jax.random.randint(splits[4], (NPAIR, 2), 0, NOCC), jax.random.fold_in(splits[4], 1), 0, NOCC - 1).astype(jnp.int32),
        "pair_state": place_ends(jax.random.randint(splits[5], (NPAIR,), 0, NSTATE), jax.random.fold_in(splits[5], 1), 0, NSTATE - 1).astype(jnp.int32),
        "state_shift": jnp.clip(jnp.exp(jax.random.uniform(splits[6], (NSTATE,), jnp.float32, math.log(0.1), math.log(1.0))), 0.1, 1.0),
    }


def reference(factors, occ_energy, vir_energy, slab_orbitals, pair_list, pair_state, state_shift):
    blocks = []
    for pair in range(NPAIR):
        first = pair_list[pair, 0]
        second = pair_list[pair, 1]
        left = lax.dynamic_index_in_dim(factors, first, 1, keepdims=False)
        right = lax.dynamic_index_in_dim(factors, second, 1, keepdims=False)
        kernel = lax.dot_general(left, right, (((0,), (0,)), ((), ())), preferred_element_type=jnp.float32)
        e_first = occ_energy[slab_orbitals[first]]
        e_second = occ_energy[slab_orbitals[second]]
        denom = (vir_energy[:, None] + vir_energy[None, :]) - e_first - e_second + state_shift[pair_state[pair]]
        blocks.append(-kernel / denom)
    return jnp.stack(blocks)
```

```python
import functools

import jax
import jax.numpy as jnp
from jax import lax
from jax.experimental import pallas as pl
from jax.experimental.pallas import tpu as pltpu
from jax.sharding import PartitionSpec as P

MESH = pl.DeviceIdType.MESH
LAG_SOURCE = 1
LAG_RING = 2


def ring_place(row, n_row):
    half = n_row // 2
    return jnp.where(row < half, row, n_row - 1 + half - row)


def gather_kernel(n_row, n_col, x_ref, a_ref, b_ref, recv_a, recv_b, send_row, send_up, send_down, send_pair, send_ring):
    n_chip = n_col // 2
    depth = x_ref.shape[1]
    wide = a_ref.shape[2]
    narrow = b_ref.shape[2]
    row = lax.axis_index("row")
    col = lax.axis_index("col")
    chip = col // 2
    core = col % 2
    has_up = chip + 1 < n_chip
    has_down = chip > 0
    up = (row, lax.rem(col + 2, n_col))
    down = (row, lax.rem(col + n_col - 2, n_col))
    pair = (row, chip * 2 + 1 - core)
    source_row = (col * narrow) // wide
    inside = pl.multiple_of(col * narrow - source_row * wide, narrow)
    place = ring_place(row, n_row)
    hop = lax.rem(place - ring_place(source_row, n_row) + n_row, n_row)
    after = (ring_place(lax.rem(place + 1, n_row), n_row), col)
    before = (ring_place(lax.rem(place + n_row - 1, n_row), n_row), col)

    barrier = pltpu.get_barrier_semaphore()
    for step in range(1, n_row):
        pl.semaphore_signal(barrier, inc=1, device_id=(row ^ step, col), device_id_type=MESH)
    pl.semaphore_signal(barrier, inc=1, device_id=pair, device_id_type=MESH)

    @pl.when(has_up)
    def _():
        pl.semaphore_signal(barrier, inc=1, device_id=up, device_id_type=MESH)

    @pl.when(has_down)
    def _():
        pl.semaphore_signal(barrier, inc=1, device_id=down, device_id_type=MESH)

    pl.semaphore_wait(barrier, n_row + has_up.astype(jnp.int32) + has_down.astype(jnp.int32))

    def a_piece(index):
        return a_ref.at[:, pl.ds(pl.multiple_of(index * depth, depth), depth), :]

    def b_piece(index):
        return b_ref.at[:, pl.ds(pl.multiple_of(index * depth, depth), depth), :]

    def a_columns(index):
        return a_ref.at[:, pl.ds(pl.multiple_of(index * depth, depth), depth), pl.ds(inside, narrow)]

    def x_columns(target):
        return x_ref.at[:, :, pl.ds(pl.multiple_of(target * wide, wide), wide)]

    mine = col * n_row + row

    def row_copy(step):
        return pltpu.make_async_remote_copy(
            src_ref=x_columns(row ^ step), dst_ref=a_piece(mine), send_sem=send_row.at[step],
            recv_sem=recv_a.at[mine], device_id=(row ^ step, col), device_id_type=MESH)

    def line_copy(index, sems, target):
        return pltpu.make_async_remote_copy(
            src_ref=a_piece(index), dst_ref=a_piece(index), send_sem=sems.at[index],
            recv_sem=recv_a.at[index], device_id=target, device_id_type=MESH)

    def ring_copy(source, index, target):
        return pltpu.make_async_remote_copy(
            src_ref=source, dst_ref=b_piece(index), send_sem=send_ring.at[index],
            recv_sem=recv_b.at[index], device_id=target, device_id_type=MESH)

    def own_b_copy(index):
        return pltpu.make_async_copy(a_columns(index), b_piece(index), recv_b.at[index])

    def arrived_a(index):
        pltpu.make_async_copy(a_piece(index), a_piece(index), recv_a.at[index]).wait()

    def arrived_b(index):
        pltpu.make_async_copy(b_piece(index), b_piece(index), recv_b.at[index]).wait()

    pltpu.make_async_copy(x_columns(row), a_piece(mine), recv_a.at[mine]).start()
    for step in range(1, n_row):
        row_copy(step).start()

    total = n_chip * n_row

    def number(chip_at, core_at, step):
        return (chip_at * 2 + core_at) * n_row + (row ^ step)

    def ring_number(chip_at, core_at, step):
        return (chip_at * 2 + core_at) * n_row + (source_row ^ step)

    def each_chip(at, act):
        away = at // n_row
        step = lax.rem(at, n_row)

        @pl.when(away == 0)
        def _():
            act(chip, step, True, True)

        @pl.when((away > 0) & (chip + away < n_chip))
        def _():
            act(chip + away, step, False, True)

        @pl.when((away > 0) & (chip - away >= 0))
        def _():
            act(chip - away, step, True, False)

    def line(chip_at, step, go_up, go_down):
        index = number(chip_at, core, step)
        arrived_a(index)
        if go_up:
            @pl.when(has_up)
            def _():
                line_copy(index, send_up, up).start()
        if go_down:
            @pl.when(has_down)
            def _():
                line_copy(index, send_down, down).start()
        line_copy(index, send_pair, pair).start()

    def line_end(chip_at, step, go_up, go_down):
        index = number(chip_at, core, step)
        if go_up:
            @pl.when(has_up)
            def _():
                line_copy(index, send_up, up).wait_send()
        if go_down:
            @pl.when(has_down)
            def _():
                line_copy(index, send_down, down).wait_send()
        line_copy(index, send_pair, pair).wait_send()

    def source(chip_at, step, go_up, go_down):
        arrived_a(number(chip_at, 1 - core, step))

        @pl.when(hop == 0)
        def _():
            for core_at, target in ((0, after), (1, before)):
                index = number(chip_at, core_at, step)
                ring_copy(a_columns(index), index, target).start()
                own_b_copy(index).start()

    def ring(chip_at, step, go_up, go_down):
        for core_at, target, last in ((0, after, n_row - 1), (1, before, 1)):
            index = ring_number(chip_at, core_at, step)
            arrived_b(index)

            @pl.when((hop != 0) & (hop != last))
            def _():
                ring_copy(b_piece(index), index, target).start()

    def ring_end(chip_at, step, go_up, go_down):
        for core_at, target, last in ((0, after, n_row - 1), (1, before, 1)):
            index = ring_number(chip_at, core_at, step)

            @pl.when(hop != last)
            def _():
                ring_copy(b_piece(index), index, target).wait_send()

    def turn(at, carry):
        @pl.when(at < total)
        def _():
            each_chip(at, line)

        @pl.when((at >= LAG_SOURCE) & (at < total + LAG_SOURCE))
        def _():
            each_chip(at - LAG_SOURCE, source)

        @pl.when(at >= LAG_RING)
        def _():
            each_chip(at - LAG_RING, ring)

        return carry

    lax.fori_loop(0, total + LAG_RING, turn, 0)

    for step in range(1, n_row):
        row_copy(step).wait_send()

    def end(at, carry):
        each_chip(at, line_end)
        each_chip(at, ring_end)
        return carry

    lax.fori_loop(0, total, end, 0)


def gather(x, n_row, n_col):
    nocc, depth, nvir = x.shape
    total = depth * n_row * n_col
    pieces = n_row * n_col
    return pl.pallas_call(
        functools.partial(gather_kernel, n_row, n_col),
        out_shape=(
            jax.ShapeDtypeStruct((nocc, total, nvir // n_row), x.dtype),
            jax.ShapeDtypeStruct((nocc, total, nvir // n_col), x.dtype),
        ),
        in_specs=[pl.BlockSpec(memory_space=pl.ANY)],
        out_specs=(pl.BlockSpec(memory_space=pl.ANY), pl.BlockSpec(memory_space=pl.ANY)),
        scratch_shapes=[
            pltpu.SemaphoreType.DMA((pieces,)),
            pltpu.SemaphoreType.DMA((pieces,)),
            pltpu.SemaphoreType.DMA((n_row,)),
            pltpu.SemaphoreType.DMA((pieces,)),
            pltpu.SemaphoreType.DMA((pieces,)),
            pltpu.SemaphoreType.DMA((pieces,)),
            pltpu.SemaphoreType.DMA((pieces,)),
        ],
        compiler_params=pltpu.CompilerParams(collective_id=0, has_side_effects=True),
        name="gather",
    )(x)


def product_kernel(occ_ref, slab_ref, pair_ref, state_ref, shift_ref, va_ref, vb_ref, a_ref, b_ref, out_ref, acc_ref):
    at = pl.program_id(0)
    nocc = a_ref.shape[0]

    @pl.when(at == 0)
    def _():
        acc_ref[...] = jnp.zeros_like(acc_ref)

    for i in range(nocc):
        left = a_ref[i]
        for j in range(nocc):
            acc_ref[i * nocc + j] += lax.dot_general(
                left, b_ref[j], (((0,), (0,)), ((), ())), preferred_element_type=jnp.float32)

    @pl.when(at == pl.num_programs(0) - 1)
    def _():
        @pl.loop(0, out_ref.shape[0])
        def _(p):
            first = pair_ref[p, 0]
            second = pair_ref[p, 1]
            e_first = occ_ref[slab_ref[first]]
            e_second = occ_ref[slab_ref[second]]
            shift = shift_ref[state_ref[p]]
            denom = (va_ref[...] + vb_ref[...]) - e_first - e_second + shift
            out_ref[p] = -acc_ref[first * nocc + second] / denom


def product(a, b, occ_energy, slab_orbitals, pair_list, pair_state, state_shift, vir_a, vir_b, steps):
    nocc, total, wide = a.shape
    narrow = b.shape[2]
    npair = pair_list.shape[0]
    chunk = total // steps
    smem = pl.BlockSpec(memory_space=pltpu.SMEM)
    return pl.pallas_call(
        product_kernel,
        grid=(steps,),
        out_shape=jax.ShapeDtypeStruct((npair, wide, narrow), jnp.float32),
        in_specs=[smem] * 5 + [
            pl.BlockSpec((wide, 1), lambda s: (0, 0)),
            pl.BlockSpec((1, narrow), lambda s: (0, 0)),
            pl.BlockSpec((nocc, chunk, wide), lambda s: (0, s, 0)),
            pl.BlockSpec((nocc, chunk, narrow), lambda s: (0, s, 0)),
        ],
        out_specs=pl.BlockSpec((npair, wide, narrow), lambda s: (0, 0, 0)),
        scratch_shapes=[pltpu.VMEM((nocc * nocc, wide, narrow), jnp.float32)],
        compiler_params=pltpu.CompilerParams(vmem_limit_bytes=52 * 1024 * 1024),
        name="product",
    )(occ_energy, slab_orbitals, pair_list, pair_state, state_shift, vir_a, vir_b, a, b)


def shards(factors, occ_energy, vir_energy, slab_orbitals, pair_list, pair_state, state_shift):
    n_row = lax.axis_size("row")
    n_col = lax.axis_size("col")
    nvir = factors.shape[2]
    rows_a = nvir // n_row
    cols_b = nvir // n_col
    block_a, block_b = gather(factors.transpose(1, 0, 2), n_row, n_col)
    vir_a = lax.dynamic_slice_in_dim(vir_energy, lax.axis_index("row") * rows_a, rows_a)
    vir_b = lax.dynamic_slice_in_dim(vir_energy, lax.axis_index("col") * cols_b, cols_b)
    return product(block_a, block_b, occ_energy, slab_orbitals, pair_list, pair_state, state_shift,
                   vir_a[:, None], vir_b[None, :], 2 * n_col)


def solution(mesh):
    placed = (P(("row", "col"), None, None), P(), P(), P(), P(), P(), P())
    return jax.shard_map(
        shards, mesh=mesh, in_specs=placed, out_specs=P(None, "row", "col"), check_vma=False
    )
```

```python
import functools

import jax
import jax.numpy as jnp
from jax import lax
from jax.experimental import pallas as pl
from jax.experimental.pallas import tpu as pltpu
from jax.sharding import PartitionSpec as P

MESH = pl.DeviceIdType.MESH
LAG_SOURCE = 1
LAG_RING = 5


def ring_place(row, n_row):
    half = n_row // 2
    return jnp.where(row < half, row, n_row - 1 + half - row)


def gather_kernel(n_row, n_col, x_ref, a_ref, b_ref, recv_a, recv_b, send_row, send_up, send_down, send_pair, send_ring):
    n_chip = n_col // 2
    depth = x_ref.shape[1]
    wide = a_ref.shape[2]
    narrow = b_ref.shape[2]
    row = lax.axis_index("row")
    col = lax.axis_index("col")
    chip = col // 2
    core = col % 2
    has_up = chip + 1 < n_chip
    has_down = chip > 0
    up = (row, lax.rem(col + 2, n_col))
    down = (row, lax.rem(col + n_col - 2, n_col))
    pair = (row, chip * 2 + 1 - core)
    source_row = (col * narrow) // wide
    inside = pl.multiple_of(col * narrow - source_row * wide, narrow)
    place = ring_place(row, n_row)
    hop = lax.rem(place - ring_place(source_row, n_row) + n_row, n_row)
    after = (ring_place(lax.rem(place + 1, n_row), n_row), col)
    before = (ring_place(lax.rem(place + n_row - 1, n_row), n_row), col)

    barrier = pltpu.get_barrier_semaphore()
    for step in range(1, n_row):
        pl.semaphore_signal(barrier, inc=1, device_id=(row ^ step, col), device_id_type=MESH)
    pl.semaphore_signal(barrier, inc=1, device_id=pair, device_id_type=MESH)

    @pl.when(has_up)
    def _():
        pl.semaphore_signal(barrier, inc=1, device_id=up, device_id_type=MESH)

    @pl.when(has_down)
    def _():
        pl.semaphore_signal(barrier, inc=1, device_id=down, device_id_type=MESH)

    pl.semaphore_wait(barrier, n_row + has_up.astype(jnp.int32) + has_down.astype(jnp.int32))

    def a_piece(index):
        return a_ref.at[:, pl.ds(pl.multiple_of(index * depth, depth), depth), :]

    def b_piece(index):
        return b_ref.at[:, pl.ds(pl.multiple_of(index * depth, depth), depth), :]

    def a_columns(index):
        return a_ref.at[:, pl.ds(pl.multiple_of(index * depth, depth), depth), pl.ds(inside, narrow)]

    def x_columns(target):
        return x_ref.at[:, :, pl.ds(pl.multiple_of(target * wide, wide), wide)]

    mine = col * n_row + row

    def row_copy(step):
        return pltpu.make_async_remote_copy(
            src_ref=x_columns(row ^ step), dst_ref=a_piece(mine), send_sem=send_row.at[step],
            recv_sem=recv_a.at[mine], device_id=(row ^ step, col), device_id_type=MESH)

    def line_copy(index, sems, target):
        return pltpu.make_async_remote_copy(
            src_ref=a_piece(index), dst_ref=a_piece(index), send_sem=sems.at[index],
            recv_sem=recv_a.at[index], device_id=target, device_id_type=MESH)

    def ring_copy(source, index, target):
        return pltpu.make_async_remote_copy(
            src_ref=source, dst_ref=b_piece(index), send_sem=send_ring.at[index],
            recv_sem=recv_b.at[index], device_id=target, device_id_type=MESH)

    def own_b_copy(index):
        return pltpu.make_async_copy(a_columns(index), b_piece(index), recv_b.at[index])

    def arrived_a(index):
        pltpu.make_async_copy(a_piece(index), a_piece(index), recv_a.at[index]).wait()

    def arrived_b(index):
        pltpu.make_async_copy(b_piece(index), b_piece(index), recv_b.at[index]).wait()

    pltpu.make_async_copy(x_columns(row), a_piece(mine), recv_a.at[mine]).start()
    for step in range(1, n_row):
        row_copy(step).start()

    total = n_chip * n_row

    def number(chip_at, core_at, step):
        return (chip_at * 2 + core_at) * n_row + (row ^ step)

    def ring_number(chip_at, core_at, step):
        return (chip_at * 2 + core_at) * n_row + (source_row ^ step)

    def each_chip(at, act):
        away = at // n_row
        step = lax.rem(at, n_row)

        @pl.when(away == 0)
        def _():
            act(chip, step, True, True)

        @pl.when((away > 0) & (chip + away < n_chip))
        def _():
            act(chip + away, step, False, True)

        @pl.when((away > 0) & (chip - away >= 0))
        def _():
            act(chip - away, step, True, False)

    def line(chip_at, step, go_up, go_down):
        index = number(chip_at, core, step)
        arrived_a(index)
        if go_up:
            @pl.when(has_up)
            def _():
                line_copy(index, send_up, up).start()
        if go_down:
            @pl.when(has_down)
            def _():
                line_copy(index, send_down, down).start()
        line_copy(index, send_pair, pair).start()

    def line_end(chip_at, step, go_up, go_down):
        index = number(chip_at, core, step)
        if go_up:
            @pl.when(has_up)
            def _():
                line_copy(index, send_up, up).wait_send()
        if go_down:
            @pl.when(has_down)
            def _():
                line_copy(index, send_down, down).wait_send()
        line_copy(index, send_pair, pair).wait_send()

    def source(chip_at, step, go_up, go_down):
        arrived_a(number(chip_at, 1 - core, step))

        @pl.when(hop == 0)
        def _():
            for core_at, target in ((0, after), (1, before)):
                index = number(chip_at, core_at, step)
                ring_copy(a_columns(index), index, target).start()
                own_b_copy(index).start()

    def ring(chip_at, step, go_up, go_down):
        for core_at, target, last in ((0, after, n_row - 1), (1, before, 1)):
            index = ring_number(chip_at, core_at, step)
            arrived_b(index)

            @pl.when((hop != 0) & (hop != last))
            def _():
                ring_copy(b_piece(index), index, target).start()

    def ring_end(chip_at, step, go_up, go_down):
        for core_at, target, last in ((0, after, n_row - 1), (1, before, 1)):
            index = ring_number(chip_at, core_at, step)

            @pl.when(hop != last)
            def _():
                ring_copy(b_piece(index), index, target).wait_send()

    def turn(at, carry):
        @pl.when(at < total)
        def _():
            each_chip(at, line)

        @pl.when((at >= LAG_SOURCE) & (at < total + LAG_SOURCE))
        def _():
            each_chip(at - LAG_SOURCE, source)

        @pl.when(at >= LAG_RING)
        def _():
            each_chip(at - LAG_RING, ring)

        return carry

    lax.fori_loop(0, total + LAG_RING, turn, 0)

    for step in range(1, n_row):
        row_copy(step).wait_send()

    def end(at, carry):
        each_chip(at, line_end)
        each_chip(at, ring_end)
        return carry

    lax.fori_loop(0, total, end, 0)


def gather(x, n_row, n_col):
    nocc, depth, nvir = x.shape
    total = depth * n_row * n_col
    pieces = n_row * n_col
    return pl.pallas_call(
        functools.partial(gather_kernel, n_row, n_col),
        out_shape=(
            jax.ShapeDtypeStruct((nocc, total, nvir // n_row), x.dtype),
            jax.ShapeDtypeStruct((nocc, total, nvir // n_col), x.dtype),
        ),
        in_specs=[pl.BlockSpec(memory_space=pl.ANY)],
        out_specs=(pl.BlockSpec(memory_space=pl.ANY), pl.BlockSpec(memory_space=pl.ANY)),
        scratch_shapes=[
            pltpu.SemaphoreType.DMA((pieces,)),
            pltpu.SemaphoreType.DMA((pieces,)),
            pltpu.SemaphoreType.DMA((n_row,)),
            pltpu.SemaphoreType.DMA((pieces,)),
            pltpu.SemaphoreType.DMA((pieces,)),
            pltpu.SemaphoreType.DMA((pieces,)),
            pltpu.SemaphoreType.DMA((pieces,)),
        ],
        compiler_params=pltpu.CompilerParams(collective_id=0, has_side_effects=True),
        name="gather",
    )(x)


def product_kernel(occ_ref, slab_ref, pair_ref, state_ref, shift_ref, va_ref, vb_ref, a_ref, b_ref, out_ref, acc_ref):
    at = pl.program_id(0)
    nocc = a_ref.shape[0]

    @pl.when(at == 0)
    def _():
        acc_ref[...] = jnp.zeros_like(acc_ref)

    for i in range(nocc):
        left = a_ref[i]
        for j in range(nocc):
            acc_ref[i * nocc + j] += lax.dot_general(
                left, b_ref[j], (((0,), (0,)), ((), ())), preferred_element_type=jnp.float32)

    @pl.when(at == pl.num_programs(0) - 1)
    def _():
        @pl.loop(0, out_ref.shape[0])
        def _(p):
            first = pair_ref[p, 0]
            second = pair_ref[p, 1]
            e_first = occ_ref[slab_ref[first]]
            e_second = occ_ref[slab_ref[second]]
            shift = shift_ref[state_ref[p]]
            denom = (va_ref[...] + vb_ref[...]) - e_first - e_second + shift
            out_ref[p] = -acc_ref[first * nocc + second] / denom


def product(a, b, occ_energy, slab_orbitals, pair_list, pair_state, state_shift, vir_a, vir_b, steps):
    nocc, total, wide = a.shape
    narrow = b.shape[2]
    npair = pair_list.shape[0]
    chunk = total // steps
    smem = pl.BlockSpec(memory_space=pltpu.SMEM)
    return pl.pallas_call(
        product_kernel,
        grid=(steps,),
        out_shape=jax.ShapeDtypeStruct((npair, wide, narrow), jnp.float32),
        in_specs=[smem] * 5 + [
            pl.BlockSpec((wide, 1), lambda s: (0, 0)),
            pl.BlockSpec((1, narrow), lambda s: (0, 0)),
            pl.BlockSpec((nocc, chunk, wide), lambda s: (0, s, 0)),
            pl.BlockSpec((nocc, chunk, narrow), lambda s: (0, s, 0)),
        ],
        out_specs=pl.BlockSpec((npair, wide, narrow), lambda s: (0, 0, 0)),
        scratch_shapes=[pltpu.VMEM((nocc * nocc, wide, narrow), jnp.float32)],
        compiler_params=pltpu.CompilerParams(vmem_limit_bytes=52 * 1024 * 1024),
        name="product",
    )(occ_energy, slab_orbitals, pair_list, pair_state, state_shift, vir_a, vir_b, a, b)


def shards(factors, occ_energy, vir_energy, slab_orbitals, pair_list, pair_state, state_shift):
    n_row = lax.axis_size("row")
    n_col = lax.axis_size("col")
    nvir = factors.shape[2]
    rows_a = nvir // n_row
    cols_b = nvir // n_col
    block_a, block_b = gather(factors.transpose(1, 0, 2), n_row, n_col)
    vir_a = lax.dynamic_slice_in_dim(vir_energy, lax.axis_index("row") * rows_a, rows_a)
    vir_b = lax.dynamic_slice_in_dim(vir_energy, lax.axis_index("col") * cols_b, cols_b)
    return product(block_a, block_b, occ_energy, slab_orbitals, pair_list, pair_state, state_shift,
                   vir_a[:, None], vir_b[None, :], 2 * n_col)


def solution(mesh):
    placed = (P(("row", "col"), None, None), P(), P(), P(), P(), P(), P())
    return jax.shard_map(
        shards, mesh=mesh, in_specs=placed, out_specs=P(None, "row", "col"), check_vma=False
    )
```
